32 devices in a mesh: grp: 2 (over y), pos: 16 (over z, x, core).
Axes of the slice: x: 2, y: 2, z: 4, core: 2. Of those that a mesh axis runs over, the one named last changes fastest.
Arguments:
- sequences: int32 [1024, 128], P(('grp', 'pos')), parts along dimension 0, may hold values from 0 to 20
- fields: float32 [1024, 21], P(('grp', 'pos')), parts along dimension 0, may hold values from -3 to 3
- band_coupling: float32 [1024, 16, 441], P(('grp', 'pos')), parts along dimension 0, may hold values from -1 to 1
- contact_coupling: float32 [32, 16, 8, 441], P(('grp', 'pos')), parts along dimension 0, may hold values from -1.6 to 1.6
- slot_start: int32 [32, 16, 8], P(('grp', 'pos')), parts along dimension 0, may hold values from -1 to 31, as said below
- slot_end: int32 [32, 16, 8], P(('grp', 'pos')), parts along dimension 0, may hold values from -1 to 31, as said below
- seq_weight: float32 [256], P('grp'), parts along dimension 0, may hold values from 0.02 to 0.25
Outputs:
- grad_band: float32 [1024, 16, 441], P(('grp', 'pos')), parts along dimension 0
- grad_contact: float32 [32, 16, 8, 441], P(('grp', 'pos')), parts along dimension 0
- grad_field: float32 [1024, 21], P(('grp', 'pos')), parts along dimension 0
The draws below stay inside these ranges and needn't reach their ends.
There are 2 independent parts, one for each index of `grp`. The reference program is written for one: setup_inputs(seed, part) draws one part's arguments, and reference() takes and returns one part's arrays. A program takes and returns all parts, laid end to end along the dimension named above; each array names one. Nothing has to cross between parts.
Inputs may be any that keep to these rules, and one draw needn't show every extreme that they name: `slot_start`: entry [d, e, c] is the position, within the block of 32 positions of device d, where contact slot c from device d to device e begins, or -1 where that slot is empty. `slot_end`: entry [e, d, c] is the position, within the block of device e, where the contact of slot c from device d to device e ends; it is -1 exactly where slot_start[d, e, c] is -1, and a contact never joins a position to itself.
All inputs are finite; a program needn't handle non-finite values.
Results may differ from the reference program's by a relative error of at most 0.0001.
Values sent between devices are 32-bit elements; how exact they have to be, the bound alone decides.
A program may use at most 128 MiB of HBM per device.

```python
import math
import jax
import jax.numpy as jnp
import numpy as np
from jax import lax

STATES = 21
BAND = 16
POS_DEV = 32
SEQS = 128
RESIDUES = 512
SLOTS = 8
N_POS = 16


def slot_graph(key):
    fill_key, level_key, start_key, end_key = jax.random.split(key, 4)
    limits = jax.random.randint(fill_key, (N_POS,), 2, 9)
    levels = jax.random.randint(level_key, (N_POS, N_POS, SLOTS), 0, 8)
    used = levels < limits[None, :, None]
    starts = jax.random.randint(start_key, (N_POS, N_POS, SLOTS), 0, POS_DEV)
    ends = jax.random.randint(end_key, (N_POS, N_POS, SLOTS), 0, POS_DEV)
    devices = jnp.arange(N_POS, dtype=jnp.int32)
    same = (devices[:, None, None] == devices[None, :, None]) & (starts == ends)
    ends = jnp.where(same, (ends + 1) % POS_DEV, ends)
    sending = jnp.where(used, starts, -1).astype(jnp.int32)
    arriving = jnp.transpose(jnp.where(used, ends, -1), (1, 0, 2)).astype(jnp.int32)
    return (sending, arriving)


def draw_slot_start(key, part):
    return slot_graph(key)[0]


def draw_slot_end(key, part):
    return slot_graph(key)[1]


def with_ends(entries, rng, smallest, largest):
    index_at = [jax.random.randint(jax.random.fold_in(rng, axis), (), 0, length) for axis, length in enumerate(entries.shape)]
    main_axis = entries.shape.index(max(entries.shape))
    neighbour = index_at[:main_axis] + [(index_at[main_axis] + 1) % entries.shape[main_axis]] + index_at[main_axis + 1:]
    return entries.at[tuple(index_at)].set(smallest).at[tuple(neighbour)].set(largest)


def block_levels(own_key, shape, cuts, smallest, top_value):
    gain = 1.0
    for position, parts in cuts:
        steps = jax.random.uniform(jax.random.fold_in(jax.random.fold_in(own_key, 6), position), (parts,), jnp.float32, smallest / len(cuts), top_value / len(cuts))
        gain = gain * jnp.repeat(jnp.exp(steps), shape[position] // parts).reshape((-1,) + (1,) * (len(shape) - 1 - position))
    return gain


def rank_bounds(amount, slope):
    portions = [(1 << 20) // math.isqrt(rank ** slope) + 1 for rank in range(1, amount + 1)]
    deviation = 1 + sum(portions) // (1 << 30)
    return np.cumsum(np.array([max(1, weight // deviation) for weight in portions]))


def ranked_ids(own_key, shape, amount, skew):
    table = rank_bounds(amount, skew)
    lot = jax.random.randint(jax.random.fold_in(own_key, 1), shape, 0, int(table[amount - 1]))
    rank = jnp.searchsorted(jnp.asarray(table, jnp.int32), lot, side="right")
    return jax.random.permutation(jax.random.fold_in(own_key, 2), amount)[rank].astype(jnp.int32)


def bell_draw(stream_key, extent, deviation, bound, shards=(), held_as=jnp.bfloat16):
    loudness = block_levels(stream_key, extent, shards, -0.22, 0.18) if shards else 1.0
    array = jax.random.normal(stream_key, extent, jnp.float32) * deviation * loudness
    return jnp.minimum(jnp.maximum(array, -bound), bound).astype(held_as)


def setup_inputs(seed: int = 0, part: int = 0) -> dict:
    seeds = jax.random.split(jax.random.key(seed), 8)
    own_keys = jax.random.split(jax.random.fold_in(seeds[7], part), 8)
    sequences = with_ends(ranked_ids(own_keys[0], (RESIDUES, SEQS), STATES, 2), jax.random.fold_in(own_keys[0], 3), 0, STATES - 1).astype(jnp.int32)
    fields = bell_draw(own_keys[1], (RESIDUES, STATES), 1.0, 3.0, ((0, 16),), jnp.float32)
    band_coupling = bell_draw(own_keys[2], (RESIDUES, BAND, STATES * STATES), 0.25, 1.0, ((0, 16),), jnp.float32)
    contact_coupling = bell_draw(own_keys[3], (N_POS, N_POS, SLOTS, STATES * STATES), 0.4, 1.6, ((0, 16),), jnp.float32)
    slot_start = draw_slot_start(jax.random.fold_in(jax.random.fold_in(seeds[7], part), 71), part)
    slot_end = draw_slot_end(jax.random.fold_in(jax.random.fold_in(seeds[7], part), 71), part)
    seq_weight = jnp.clip(jnp.exp(jax.random.uniform(own_keys[6], (SEQS,), jnp.float32, math.log(0.02), math.log(0.25))), 0.02, 0.25)
    return {"sequences": sequences, "fields": fields, "band_coupling": band_coupling, "contact_coupling": contact_coupling, "slot_start": slot_start, "slot_end": slot_end, "seq_weight": seq_weight}


precise = lax.Precision.HIGHEST

def hot_states(sequences, states):
    levels = jnp.arange(states, dtype=jnp.int32)
    return (sequences[:, None, :] == levels[None, :, None]).astype(jnp.float32)

def reference(sequences, fields, band_coupling, contact_coupling, slot_start, slot_end, seq_weight):
    one_hot = hot_states(sequences, STATES)
    band_blocks = band_coupling.reshape(RESIDUES, BAND, STATES, STATES)
    logits = jnp.broadcast_to(fields[:, :, None], one_hot.shape).astype(jnp.float32)
    for offset in range(1, BAND + 1):
        kept_rows = RESIDUES - offset
        blocks_now = band_blocks[:kept_rows, offset - 1]
        lifted = jnp.einsum('iab,ian->ibn', blocks_now, one_hot[:kept_rows], precision=precise)
        pulled = jnp.einsum('iab,ibn->ian', blocks_now, one_hot[offset:], precision=precise)
        logits = logits.at[offset:].add(lifted).at[:kept_rows].add(pulled)
    devices = jnp.arange(N_POS, dtype=jnp.int32)
    live_slots = (slot_start >= 0).astype(jnp.float32)
    arrive = jnp.transpose(slot_end, (1, 0, 2))
    sources = devices[:, None, None] * POS_DEV + jnp.maximum(slot_start, 0)
    targets = devices[None, :, None] * POS_DEV + jnp.maximum(arrive, 0)
    per_device = N_POS * SLOTS
    live_rows = live_slots.reshape(N_POS, per_device)
    coupling = contact_coupling.reshape(N_POS, per_device, STATES, STATES) * live_rows[:, :, None, None]
    sources = sources.reshape(N_POS, per_device).astype(jnp.int32)
    targets = targets.reshape(N_POS, per_device).astype(jnp.int32)

    def add_block(running, inputs):
        blocks, from_rows, to_rows = inputs
        outward = jnp.einsum('sab,san->sbn', blocks, one_hot[from_rows], precision=precise)
        inward = jnp.einsum('sab,sbn->san', blocks, one_hot[to_rows], precision=precise)
        return (running.at[to_rows].add(outward).at[from_rows].add(inward), None)
    logits, _ = lax.scan(add_block, logits, (coupling, sources, targets))
    exp_logits = jnp.exp(logits)
    probability = exp_logits / lax.optimization_barrier(jnp.sum(exp_logits, axis=1, keepdims=True))
    residual = seq_weight[None, None, :] * (probability - one_hot)
    grad_field = lax.optimization_barrier(jnp.sum(residual, axis=2))
    pieces = []
    for offset in range(1, BAND + 1):
        kept_rows = RESIDUES - offset
        gradient = jnp.einsum('ian,ibn->iab', residual[:kept_rows], one_hot[offset:], precision=precise)
        gradient = gradient + jnp.einsum('ian,ibn->iab', one_hot[:kept_rows], residual[offset:], precision=precise)
        pieces.append(jnp.concatenate([gradient, jnp.zeros((offset, STATES, STATES), jnp.float32)], 0))
    grad_band = jnp.stack(pieces, 1).reshape(RESIDUES, BAND, STATES * STATES)

    def block_grad(inputs):
        live, from_rows, to_rows = inputs
        gradient = jnp.einsum('san,sbn->sab', residual[from_rows], one_hot[to_rows], precision=precise)
        gradient = gradient + jnp.einsum('san,sbn->sab', one_hot[from_rows], residual[to_rows], precision=precise)
        return gradient * live[:, None, None]
    grad_contact = lax.map(block_grad, (live_rows, sources, targets)).reshape(N_POS, N_POS, SLOTS, STATES * STATES)
    return (grad_band, grad_contact, grad_field)
```

```python
import functools

import jax
import jax.numpy as jnp
import numpy as np
from jax import lax
from jax.experimental import pallas as pl
from jax.experimental.pallas import tpu as pltpu
from jax.sharding import PartitionSpec as P

LANES = 128
SUB = 8
PAD = 32
PER = LANES // PAD
f32, bf16, i32 = jnp.float32, jnp.bfloat16, jnp.int32


def split(x):
    hi = x.astype(bf16)
    return hi, (x - hi.astype(f32)).astype(bf16)


def dot(a, b):
    return jnp.dot(a, b, preferred_element_type=f32)


def dot_nt(a, b):
    return lax.dot_general(a, b, (((1,), (1,)), ((), ())), preferred_element_type=f32)


def lookup(table, index):
    return jnp.take_along_axis(table, index, axis=1, mode="promise_in_bounds")


def iota(shape, dim):
    return lax.broadcasted_iota(i32, shape, dim)


def flip_matrix(states, flat):
    per = LANES // states
    out = np.zeros((flat, -(-states // per) * LANES), np.float32)
    for b in range(states):
        for a in range(states):
            out[a * states + b, (b // per) * LANES + (b % per) * states + a] = 1.0
    return out


def kernel(
    n, depth, band,
    seq_ref, fields_ref, band_ref, contact_ref, start_ref, end_ref, weight_ref, flip_ref,
    gband_ref, gcontact_ref, gfield_ref,
    k4, t4, seql, seqh, seqx, send, recv, cont, ct4, logit, spill_out, spill_in, res, res_in,
    xhi, xlo, rj, rs, rej, dband, dcon, g4, gsend, grecv, gown,
    m_send, m_recv, g_send, g_recv, h_send, h_recv,
):
    rows, seqs = seq_ref.shape
    states = fields_ref.shape[1]
    square = states * states
    nv = k4.shape[0]
    flat = nv * LANES
    nt = t4.shape[0]
    per = LANES // states
    slots = n * depth
    tiles = slots // SUB
    me = lax.axis_index("pos")
    nxt, prv = lax.rem(me + 1, n), lax.rem(me + n - 1, n)

    def peer(k):
        return lax.rem(me + k, n)

    def remote(src, dst, ssem, rsem, to):
        return pltpu.make_async_remote_copy(
            src_ref=src, dst_ref=dst, send_sem=ssem, recv_sem=rsem,
            device_id={"pos": to}, device_id_type=pl.DeviceIdType.MESH,
        )

    def message(k):
        return remote(send.at[peer(k)], recv.at[me], m_send.at[k], m_recv.at[k], peer(k))

    def gradient(k):
        return remote(gsend.at[peer(k)], grecv.at[me], g_send.at[k], g_recv.at[k], peer(k))

    def loop(lo, hi, body):
        def step(k, c):
            body(k)
            return c
        lax.fori_loop(lo, hi, step, 0)

    def tile_of(ref, t, lo, hi):
        if depth == SUB:
            return ref[t, :, lo:hi]
        if depth > SUB:
            each = depth // SUB
            return ref[t // each, pl.ds(pl.multiple_of((t % each) * SUB, SUB), SUB), lo:hi]
        return ref[pl.ds(t * (SUB // depth), SUB // depth), :, lo:hi].reshape(SUB, hi - lo)

    def put_tile(ref, t, lo, hi, value):
        if depth == SUB:
            ref[t, :, lo:hi] = value
        elif depth > SUB:
            each = depth // SUB
            ref[t // each, pl.ds(pl.multiple_of((t % each) * SUB, SUB), SUB), lo:hi] = value
        else:
            ref[pl.ds(t * (SUB // depth), SUB // depth), :, lo:hi] = value.reshape(
                SUB // depth, depth, hi - lo
            )

    barrier = pltpu.get_barrier_semaphore()
    loop(1, n, lambda k: pl.semaphore_signal(
        barrier, inc=1, device_id={"pos": peer(k)}, device_id_type=pl.DeviceIdType.MESH))

    seq_f = seq_ref[...].astype(f32)
    seq_b = seq_f.astype(bf16)
    pick_s = (iota((rows, slots), 0) == start_ref[...]).astype(f32)
    pick_e = (iota((rows, slots), 0) == end_ref[...]).astype(f32)
    pick_st = pick_s.T.astype(bf16)
    pick_et = pick_e.T.astype(bf16)
    pick_cat = jnp.concatenate([pick_s, pick_e], axis=1).astype(bf16)
    send[:, :, flat - LANES : flat] = jnp.zeros((n, depth, LANES), f32)
    send[:, :, :square] = contact_ref[...]
    send[:, :, flat : flat + seqs] = dot(pick_st, seq_b).reshape(n, depth, seqs)
    send[:, :, flat + seqs :] = dot(pick_et, seq_b).reshape(n, depth, seqs)
    recv[me] = send[me]

    pl.semaphore_wait(barrier, n - 1)
    halo = remote(seq_ref.at[pl.ds(0, band)], seqh, h_send.at[0], h_recv.at[0], prv)
    halo.start()
    loop(1, n, lambda k: message(k).start())

    last = jnp.where(me == n - 1, 1, 0)
    row = iota((rows * band, LANES), 0)
    reach = row // band + row % band + 1
    exists = reach + last * rows < 2 * rows
    exists = jnp.where(last == 1, jnp.where(reach < rows, 1, 0), 1) == 1
    for v in range(nv):
        width = min(LANES, square - v * LANES)
        if width == LANES:
            k4[v] = jnp.where(exists, band_ref[:, v * LANES : (v + 1) * LANES], 0.0)
        else:
            k4[v] = jnp.zeros((rows * band, LANES), f32)
            k4[v, :, :width] = jnp.where(
                exists[:, :width], band_ref[:, v * LANES : v * LANES + width], 0.0)
    edge = band * band
    t4[:, :edge, :] = jnp.zeros((nt, edge, LANES), f32)
    t4[:, edge + rows * band :, :] = jnp.zeros((nt, edge, LANES), f32)

    def flip(x):
        hi, lo = split(x)
        return dot(hi, flip_ref[...]) + dot(lo, flip_ref[...])

    chunk = LANES

    def flip_band(c):
        at = pl.multiple_of(c * chunk, chunk)
        out = flip(jnp.concatenate([k4[v, pl.ds(at, chunk), :] for v in range(nv)], axis=1))
        for v in range(nt):
            t4[v, pl.ds(edge + at, chunk), :] = out[:, v * LANES : (v + 1) * LANES]
    loop(0, rows * band // chunk, flip_band)

    seql[...] = jnp.zeros(seql.shape, i32)
    seql[pl.ds(band, rows), :] = seq_ref[...]

    def lift(tables, s):
        return [lookup(tables[b // per], s + (b % per) * states) for b in range(states)]

    def pull(tables, s):
        out = []
        for a in range(states):
            at = a * states + s
            v0, v1 = a * states // LANES, (a * states + states - 1) // LANES
            got = lookup(tables[v0], at & (LANES - 1))
            if v1 != v0:
                got = jnp.where(at >= v1 * LANES, lookup(tables[v1], at & (LANES - 1)), got)
            out.append(got)
        return out

    def lift_step(j0):
        def step(w, acc):
            at = (band + j0 - w) * band + w - 1
            tables = [t4[v, pl.ds(at, SUB, stride=band), :] for v in range(nt)]
            new = lift(tables, seql[pl.ds(band + j0 - w, SUB), :])
            return tuple(x + y for x, y in zip(acc, new))
        return step

    def pull_step(i0):
        def step(w, acc):
            at = i0 * band + w - 1
            tables = [k4[v, pl.ds(at, SUB, stride=band), :] for v in range(nv)]
            new = pull(tables, seqx[pl.ds(i0 + w, SUB), :])
            return tuple(x + y for x, y in zip(acc, new))
        return step

    def lift_range(j0):
        return jnp.maximum(1, j0 - rows + 1), jnp.minimum(band, j0 + SUB - 1) + 1

    zero = jnp.zeros((SUB, seqs), f32)

    def spill_tile(t):
        j0 = rows + t * SUB
        lo, hi = lift_range(j0)
        acc = lax.fori_loop(lo, hi, lift_step(j0), (zero,) * states)
        for b in range(states):
            spill_out[b, pl.ds(pl.multiple_of(t * SUB, SUB), SUB), :] = acc[b]
    loop(0, band // SUB, spill_tile)
    spill = remote(spill_out, spill_in, h_send.at[1], h_recv.at[1], nxt)
    spill.start()

    halo.wait_recv()
    seqx[pl.ds(0, rows), :] = seq_ref[...]
    seqx[pl.ds(rows, band), :] = seqh[...]

    def logit_tile(t):
        i0 = pl.multiple_of(t * SUB, SUB)
        f = fields_ref[pl.ds(i0, SUB), :]
        acc = tuple(jnp.broadcast_to(f[:, a : a + 1], (SUB, seqs)) for a in range(states))
        lo, hi = lift_range(i0)
        acc = lax.fori_loop(lo, hi, lift_step(i0), acc)
        acc = lax.fori_loop(1, band + 1, pull_step(i0), acc)
        for a in range(states):
            logit[a, pl.ds(i0, SUB), :] = acc[a]
    loop(0, rows // SUB, logit_tile)

    loop(1, n, lambda k: message(k).wait_recv())
    flipped = flip(recv[:, :, :flat].reshape(slots, flat))
    for v in range(nt):
        ct4[v] = flipped[:, v * LANES : (v + 1) * LANES]

    def contact_tile(t):
        at = pl.multiple_of(t * SUB, SUB)
        s_end = tile_of(recv, t, flat + seqs, flat + 2 * seqs).astype(i32)
        s_start = tile_of(recv, t, flat, flat + seqs).astype(i32)
        tables = [tile_of(send, t, v * LANES, (v + 1) * LANES) for v in range(nv)]
        for a, x in enumerate(pull(tables, s_end)):
            cont[a, pl.ds(at, SUB), :] = x
        tables = [ct4[v, pl.ds(at, SUB), :] for v in range(nt)]
        for b, x in enumerate(lift(tables, s_start)):
            cont[b, pl.ds(slots + at, SUB), :] = x
    loop(0, tiles, contact_tile)

    spill.wait_recv()

    def add_contacts(a):
        hi, lo = split(cont[a])
        logit[a] = logit[a] + dot(pick_cat, hi) + dot(pick_cat, lo)
        logit[a, pl.ds(0, band), :] = logit[a, pl.ds(0, band), :] + spill_in[a]
    loop(0, states, add_contacts)

    def residual_tile(t):
        i0 = pl.multiple_of(t * SUB, SUB)
        e = [jnp.exp(logit[a, pl.ds(i0, SUB), :]) for a in range(states)]
        total = functools.reduce(lambda x, y: x + y, e)
        s = seq_ref[pl.ds(i0, SUB), :]
        w = weight_ref[...]
        lane = iota((SUB, states), 1)
        field = jnp.zeros((SUB, states), f32)
        for a in range(states):
            r = w * (e[a] / total - (s == a).astype(f32))
            res[a, pl.ds(i0, SUB), :] = r
            field = jnp.where(lane == a, jnp.sum(r, axis=1, keepdims=True), field)
        gfield_ref[pl.ds(i0, SUB), :] = field
    loop(0, rows // SUB, residual_tile)
    back = remote(res.at[:, pl.ds(0, band), :], res_in, h_send.at[2], h_recv.at[2], prv)
    back.start()

    lane = iota((SUB, LANES), 1)
    local = iota((SUB, LANES), 0)
    column = []
    for v in range(nv):
        col = lane + v * LANES
        for a in range(states - 1, 0, -1):
            if a * states <= v * LANES:
                col = lane + (v * LANES - a * states)
                first = a
                break
        else:
            first = 0
        for a in range(first + 1, states):
            if a * states < (v + 1) * LANES:
                col = jnp.where(lane + v * LANES >= a * states, lane + (v * LANES - a * states), col)
        column.append(col & (PAD - 1))

    def assemble(source, w):
        off = local + (w - 1)
        first = (w - 1) // PER
        steps = (w - 1 + SUB - 1) // PER - first
        chosen = {}

        def chosen_rows(a):
            if a not in chosen:
                x = source(a, first)
                for k in range(1, steps + 1):
                    x = jnp.where(off >= (first + k) * PER, source(a, first + k), x)
                chosen[a] = x
            return chosen[a]

        outs = []
        for v in range(nv):
            index = (off & (PER - 1)) * PAD + column[v]
            out = None
            for a in range(states):
                if a * states >= (v + 1) * LANES or (a + 1) * states <= v * LANES:
                    continue
                got = lookup(chosen_rows(a), index)
                out = got if out is None else jnp.where(lane + v * LANES >= a * states, got, out)
            outs.append(out)
        return outs

    for a in range(states):
        hi, lo = split(res[a])
        both = jnp.concatenate([hi, lo], axis=1)
        x = dot(pick_st, both)
        rs[a] = x[:, :seqs] + x[:, seqs:]
        x = dot(pick_et, both)
        rej[pl.ds(a, slots, stride=PAD), :] = x[:, :seqs] + x[:, seqs:]

    def hot_rows(s):
        return jnp.concatenate([(s == a).astype(f32) for a in range(states)], axis=0).astype(bf16)

    def hot_columns(s):
        level = iota((PAD, seqs), 0)
        return jnp.concatenate(
            [(s[r : r + 1] == level).astype(f32) for r in range(s.shape[0])], axis=0).astype(bf16)

    def from_dcon(a, v):
        return dcon[pl.ds(a * SUB, SUB), v * LANES : (v + 1) * LANES]

    def far_half(t):
        s_start = tile_of(recv, t, flat, flat + seqs).astype(i32)
        left = hot_rows(s_start)
        hi, lo = split(rej[pl.ds(pl.multiple_of(t * SUB * PAD, SUB * PAD), SUB * PAD), :])
        dcon[...] = dot_nt(left, hi) + dot_nt(left, lo)
        for v, x in enumerate(assemble(from_dcon, 1)):
            put_tile(gsend, t, v * LANES, (v + 1) * LANES, x)

    if depth == SUB:
        def far_step(k):
            far_half(peer(k))
            gradient(k).start()
        loop(1, n, far_step)
        far_half(me)
    else:
        loop(0, tiles, far_half)
        loop(1, n, lambda k: gradient(k).start())
    grecv[me] = gsend[me]

    def near_half(t):
        s_end = tile_of(recv, t, flat + seqs, flat + 2 * seqs).astype(i32)
        right = hot_columns(s_end)
        at = pl.multiple_of(t * SUB, SUB)
        hi, lo = split(rs[:, pl.ds(at, SUB), :].reshape(states * SUB, seqs))
        dcon[...] = dot_nt(hi, right) + dot_nt(lo, right)
        for v, x in enumerate(assemble(from_dcon, 1)):
            put_tile(gown, t, v * LANES, (v + 1) * LANES, x)
    loop(0, tiles, near_half)

    for a in range(states):
        rj[pl.ds(a, rows, stride=PAD), :] = res[a]
    back.wait_recv()
    for a in range(states):
        rj[pl.ds(rows * PAD + a, band, stride=PAD), :] = res_in[a]

    def columns_of(t):
        h = hot_columns(seqx[pl.ds(pl.multiple_of(t * SUB, SUB), SUB), :])
        at = pl.multiple_of(t * SUB * PAD, SUB * PAD)
        hi, lo = split(rj[pl.ds(at, SUB * PAD), :])
        xhi[pl.ds(at, SUB * PAD), :] = jnp.concatenate([h, hi], axis=1)
        xlo[pl.ds(at, SUB * PAD), :] = jnp.concatenate([h, lo], axis=1)
    loop(0, (rows + band) // SUB, columns_of)
    reached = dband.shape[1]

    def from_dband(a, v):
        return dband[pl.ds(a * SUB, SUB), v * LANES : (v + 1) * LANES]

    def band_tile(t):
        i0 = pl.multiple_of(t * SUB, SUB)
        hi, lo = split(res[:, pl.ds(i0, SUB), :].reshape(states * SUB, seqs))
        h = hot_rows(seq_ref[pl.ds(i0, SUB), :])
        at = pl.ds(pl.multiple_of((i0 + 1) * PAD, PAD), reached)
        dband[...] = dot_nt(jnp.concatenate([hi, h], axis=1), xhi[at, :]) + dot_nt(
            jnp.concatenate([lo, h], axis=1), xlo[at, :])
        for w in range(1, band + 1):
            for v, x in enumerate(assemble(from_dband, w)):
                g4[v, pl.ds(i0 * band + w - 1, SUB, stride=band), :] = x
    loop(0, rows // SUB, band_tile)

    for v in range(nv):
        width = min(LANES, square - v * LANES)
        gband_ref[:, v * LANES : v * LANES + width] = jnp.where(
            exists[:, :width], g4[v, :, :width], 0.0)

    loop(1, n, lambda k: gradient(k).wait_recv())
    gcontact_ref[...] = gown[:, :, :square] + grecv[:, :, :square]

    halo.wait_send()
    spill.wait_send()
    back.wait_send()

    def drain(k):
        message(k).wait_send()
        gradient(k).wait_send()
    loop(1, n, drain)


def on_device(sequences, fields, band_coupling, contact_coupling, slot_start, slot_end, seq_weight):
    rows, seqs = sequences.shape
    states = fields.shape[1]
    band = band_coupling.shape[1]
    n, depth = contact_coupling.shape[1:3]
    square = states * states
    slots = n * depth
    nv = -(-square // LANES)
    flat = nv * LANES
    flip = flip_matrix(states, flat)
    nt = flip.shape[1] // LANES
    near = SUB + band - 1
    reached = -(-near // SUB) * SUB * PAD
    columns = (rows - SUB + 1) * PAD + reached
    V = pltpu.VMEM
    scratch = [
        V((nv, rows * band, LANES), f32),
        V((nt, (rows + 2 * band) * band, LANES), f32),
        V((rows + 2 * band, seqs), i32),
        V((band, seqs), i32),
        V((rows + band, seqs), i32),
        V((n, depth, flat + 2 * seqs), f32),
        V((n, depth, flat + 2 * seqs), f32),
        V((states, 2 * slots, seqs), f32),
        V((nt, slots, LANES), f32),
        V((states, rows, seqs), f32),
        V((states, band, seqs), f32),
        V((states, band, seqs), f32),
        V((states, rows, seqs), f32),
        V((states, band, seqs), f32),
        V((columns, 2 * seqs), bf16),
        V((columns, 2 * seqs), bf16),
        V(((rows + band) * PAD, seqs), f32),
        V((states, slots, seqs), f32),
        V((slots * PAD, seqs), f32),
        V((states * SUB, reached), f32),
        V((states * SUB, SUB * PAD), f32),
        V((nv, rows * band, LANES), f32),
        V((n, depth, flat), f32),
        V((n, depth, flat), f32),
        V((n, depth, flat), f32),
        pltpu.SemaphoreType.DMA((n,)),
        pltpu.SemaphoreType.DMA((n,)),
        pltpu.SemaphoreType.DMA((n,)),
        pltpu.SemaphoreType.DMA((n,)),
        pltpu.SemaphoreType.DMA((3,)),
        pltpu.SemaphoreType.DMA((3,)),
    ]
    gband, gcontact, gfield = pl.pallas_call(
        functools.partial(kernel, n, depth, band),
        out_shape=(
            jax.ShapeDtypeStruct((rows * band, square), f32),
            jax.ShapeDtypeStruct((n, depth, square), f32),
            jax.ShapeDtypeStruct((rows, states), f32),
        ),
        in_specs=[pl.BlockSpec(memory_space=V)] * 8,
        out_specs=(pl.BlockSpec(memory_space=V),) * 3,
        scratch_shapes=scratch,
        compiler_params=pltpu.CompilerParams(
            collective_id=0, has_side_effects=True, vmem_limit_bytes=50 * 2**20),
    )(
        sequences,
        fields,
        band_coupling.reshape(rows * band, square),
        contact_coupling[0],
        slot_start.reshape(1, slots),
        slot_end.reshape(1, slots),
        seq_weight.reshape(1, seqs),
        jnp.asarray(flip, bf16),
    )
    return gband.reshape(rows, band, square), gcontact[None], gfield


def solution(mesh):
    in_specs = (
        P(("grp", "pos"), None),
        P(("grp", "pos"), None),
        P(("grp", "pos"), None, None),
        P(("grp", "pos"), None, None, None),
        P(("grp", "pos"), None, None),
        P(("grp", "pos"), None, None),
        P("grp"),
    )
    out_specs = (
        P(("grp", "pos"), None, None),
        P(("grp", "pos"), None, None, None),
        P(("grp", "pos"), None),
    )
    return jax.shard_map(
        on_device, mesh=mesh, in_specs=in_specs, out_specs=out_specs, check_vma=False
    )
```

```python
import functools

import jax
import jax.numpy as jnp
import numpy as np
from jax import lax
from jax.experimental import pallas as pl
from jax.experimental.pallas import tpu as pltpu
from jax.sharding import PartitionSpec as P

LANES = 128
SUB = 8
PAD = 32
PER = LANES // PAD
f32, bf16, i32 = jnp.float32, jnp.bfloat16, jnp.int32


def split(x):
    hi = x.astype(bf16)
    return hi, (x - hi.astype(f32)).astype(bf16)


def dot(a, b):
    return jnp.dot(a, b, preferred_element_type=f32)


def dot_nt(a, b):
    return lax.dot_general(a, b, (((1,), (1,)), ((), ())), preferred_element_type=f32)


def lookup(table, index):
    return jnp.take_along_axis(table, index, axis=1, mode="promise_in_bounds")


def iota(shape, dim):
    return lax.broadcasted_iota(i32, shape, dim)


def flip_matrix(states, flat):
    per = LANES // states
    out = np.zeros((flat, -(-states // per) * LANES), np.float32)
    for b in range(states):
        for a in range(states):
            out[a * states + b, (b // per) * LANES + (b % per) * states + a] = 1.0
    return out


def kernel(
    n, depth, band,
    seq_hbm, start_hbm, end_hbm, contact_hbm, band_hbm, flip_hbm, fields_hbm, weight_hbm,
    gband_ref, gcontact_ref, gfield_ref,
    k4, t4, seql, seqh, seqx, send, recv, cont, ct4, logit, spill_out, spill_in, res, res_in,
    xhi, xlo, rj, rs, rej, dband, g4, gsend, grecv, gown,
    m_send, m_recv, g_send, g_recv, h_send, h_recv,
    seq_ref, start_ref, end_ref, contact_ref, band_ref, flip_ref, fields_ref, weight_ref, in_sem,
):
    loads = [
        pltpu.make_async_copy(src, dst, in_sem.at[i])
        for i, (src, dst) in enumerate((
            (seq_hbm, seq_ref), (start_hbm, start_ref), (end_hbm, end_ref),
            (contact_hbm, contact_ref), (band_hbm, band_ref), (flip_hbm, flip_ref),
            (fields_hbm, fields_ref), (weight_hbm, weight_ref),
        ))
    ]
    for load in loads:
        load.start()
    rows, seqs = seq_ref.shape
    states = fields_ref.shape[1]
    square = states * states
    nv = k4.shape[0]
    flat = nv * LANES
    nt = t4.shape[0]
    per = LANES // states
    slots = n * depth
    tiles = slots // SUB
    me = lax.axis_index("pos")
    nxt, prv = lax.rem(me + 1, n), lax.rem(me + n - 1, n)

    def peer(k):
        return lax.rem(me + k, n)

    def remote(src, dst, ssem, rsem, to):
        return pltpu.make_async_remote_copy(
            src_ref=src, dst_ref=dst, send_sem=ssem, recv_sem=rsem,
            device_id={"pos": to}, device_id_type=pl.DeviceIdType.MESH,
        )

    def message(k):
        return remote(send.at[peer(k)], recv.at[me], m_send.at[k], m_recv.at[k], peer(k))

    def gradient(k):
        return remote(gsend.at[peer(k)], grecv.at[me], g_send.at[k], g_recv.at[k], peer(k))

    def loop(lo, hi, body, group=1, after=None):
        while (hi - lo) % group:
            group -= 1

        def step(k, c):
            for j in range(group):
                body(lo + k * group + j)
            if after is not None:
                for j in range(group):
                    after(lo + k * group + j)
            return c
        if hi - lo == group:
            step(0, 0)
        else:
            lax.fori_loop(0, (hi - lo) // group, step, 0)

    def tile_of(ref, t, lo, hi):
        if depth == SUB:
            return ref[t, :, lo:hi]
        if depth > SUB:
            each = depth // SUB
            return ref[t // each, pl.ds(pl.multiple_of((t % each) * SUB, SUB), SUB), lo:hi]
        return ref[pl.ds(t * (SUB // depth), SUB // depth), :, lo:hi].reshape(SUB, hi - lo)

    def put_tile(ref, t, lo, hi, value):
        if depth == SUB:
            ref[t, :, lo:hi] = value
        elif depth > SUB:
            each = depth // SUB
            ref[t // each, pl.ds(pl.multiple_of((t % each) * SUB, SUB), SUB), lo:hi] = value
        else:
            ref[pl.ds(t * (SUB // depth), SUB // depth), :, lo:hi] = value.reshape(
                SUB // depth, depth, hi - lo
            )

    barrier = pltpu.get_barrier_semaphore()
    loop(1, n, lambda k: pl.semaphore_signal(
        barrier, inc=1, device_id={"pos": peer(k)}, device_id_type=pl.DeviceIdType.MESH))

    for load in loads[:4]:
        load.wait()

    seq_f = seq_ref[...].astype(f32)
    seq_b = seq_f.astype(bf16)
    pick_s = (iota((rows, slots), 0) == start_ref[...]).astype(f32)
    pick_e = (iota((rows, slots), 0) == end_ref[...]).astype(f32)
    pick_st = pick_s.T.astype(bf16)
    pick_et = pick_e.T.astype(bf16)
    pick_cat = jnp.concatenate([pick_s, pick_e], axis=1).astype(bf16)
    send[:, :, flat - LANES : flat] = jnp.zeros((n, depth, LANES), f32)
    send[:, :, :square] = contact_ref[...]
    send[:, :, flat : flat + seqs] = dot(pick_st, seq_b).reshape(n, depth, seqs)
    send[:, :, flat + seqs :] = dot(pick_et, seq_b).reshape(n, depth, seqs)
    recv[me] = send[me]

    pl.semaphore_wait(barrier, n - 1)
    halo = remote(seq_ref.at[pl.ds(0, band)], seqh, h_send.at[0], h_recv.at[0], prv)
    halo.start()
    loop(1, n, lambda k: message(k).start())

    for load in loads[4:]:
        load.wait()

    last = jnp.where(me == n - 1, 1, 0)
    row = iota((rows * band, LANES), 0)
    reach = row // band + row % band + 1
    exists = reach + last * rows < 2 * rows
    exists = jnp.where(last == 1, jnp.where(reach < rows, 1, 0), 1) == 1
    for v in range(nv):
        width = min(LANES, square - v * LANES)
        if width == LANES:
            k4[v] = jnp.where(exists, band_ref[:, v * LANES : (v + 1) * LANES], 0.0)
        else:
            k4[v] = jnp.zeros((rows * band, LANES), f32)
            k4[v, :, :width] = jnp.where(
                exists[:, :width], band_ref[:, v * LANES : v * LANES + width], 0.0)
    edge = band * band
    t4[:, :edge, :] = jnp.zeros((nt, edge, LANES), f32)
    t4[:, edge + rows * band :, :] = jnp.zeros((nt, edge, LANES), f32)

    def flip(x):
        hi, lo = split(x)
        return dot(hi, flip_ref[...]) + dot(lo, flip_ref[...])

    chunk = LANES

    def flip_band(c):
        at = pl.multiple_of(c * chunk, chunk)
        out = flip(jnp.concatenate([k4[v, pl.ds(at, chunk), :] for v in range(nv)], axis=1))
        for v in range(nt):
            t4[v, pl.ds(edge + at, chunk), :] = out[:, v * LANES : (v + 1) * LANES]
    loop(0, rows * band // chunk, flip_band, 2)

    seql[...] = jnp.zeros(seql.shape, i32)
    seql[pl.ds(band, rows), :] = seq_ref[...]

    def lift(tables, s):
        return [lookup(tables[b // per], s + (b % per) * states) for b in range(states)]

    def pull(tables, s):
        out = []
        for a in range(states):
            at = a * states + s
            v0, v1 = a * states // LANES, (a * states + states - 1) // LANES
            got = lookup(tables[v0], at & (LANES - 1))
            if v1 != v0:
                got = jnp.where(at >= v1 * LANES, lookup(tables[v1], at & (LANES - 1)), got)
            out.append(got)
        return out

    def lift_step(j0):
        def step(w, acc):
            at = (band + j0 - w) * band + w - 1
            tables = [t4[v, pl.ds(at, SUB, stride=band), :] for v in range(nt)]
            new = lift(tables, seql[pl.ds(band + j0 - w, SUB), :])
            return tuple(x + y for x, y in zip(acc, new))
        return step

    def pull_step(i0):
        def step(w, acc):
            at = i0 * band + w - 1
            tables = [k4[v, pl.ds(at, SUB, stride=band), :] for v in range(nv)]
            new = pull(tables, seqx[pl.ds(i0 + w, SUB), :])
            return tuple(x + y for x, y in zip(acc, new))
        return step

    def lift_range(j0):
        return range(max(1, j0 - rows + 1), min(band, j0 + SUB - 1) + 1)

    zero = jnp.zeros((SUB, seqs), f32)

    def spill_tile(t):
        j0 = rows + t * SUB
        acc = (zero,) * states
        for w in lift_range(j0):
            acc = lift_step(j0)(w, acc)
        for b in range(states):
            spill_out[b, pl.ds(t * SUB, SUB), :] = acc[b]
    for t in range(band // SUB):
        spill_tile(t)
    spill = remote(spill_out, spill_in, h_send.at[1], h_recv.at[1], nxt)
    spill.start()

    halo.wait_recv()
    seqx[pl.ds(0, rows), :] = seq_ref[...]
    seqx[pl.ds(rows, band), :] = seqh[...]

    def logit_tile(t):
        i0 = t * SUB
        f = fields_ref[pl.ds(i0, SUB), :]
        acc = tuple(jnp.broadcast_to(f[:, a : a + 1], (SUB, seqs)) for a in range(states))
        for w in lift_range(i0):
            acc = lift_step(i0)(w, acc)
        for w in range(1, band + 1):
            acc = pull_step(i0)(w, acc)
        for a in range(states):
            logit[a, pl.ds(i0, SUB), :] = acc[a]
    for t in range(rows // SUB):
        logit_tile(t)

    loop(1, n, lambda k: message(k).wait_recv())
    flipped = flip(recv[:, :, :flat].reshape(slots, flat))
    for v in range(nt):
        ct4[v] = flipped[:, v * LANES : (v + 1) * LANES]

    def contact_tile(t):
        at = pl.multiple_of(t * SUB, SUB)
        s_end = tile_of(recv, t, flat + seqs, flat + 2 * seqs).astype(i32)
        s_start = tile_of(recv, t, flat, flat + seqs).astype(i32)
        tables = [tile_of(send, t, v * LANES, (v + 1) * LANES) for v in range(nv)]
        for a, x in enumerate(pull(tables, s_end)):
            cont[a, pl.ds(at, SUB), :] = x
        tables = [ct4[v, pl.ds(at, SUB), :] for v in range(nt)]
        for b, x in enumerate(lift(tables, s_start)):
            cont[b, pl.ds(slots + at, SUB), :] = x
    loop(0, tiles, contact_tile, 4)

    spill.wait_recv()

    def add_contacts(a):
        hi, lo = split(cont[a])
        logit[a] = logit[a] + dot(pick_cat, hi) + dot(pick_cat, lo)
        logit[a, pl.ds(0, band), :] = logit[a, pl.ds(0, band), :] + spill_in[a]
    loop(0, states, add_contacts, 7)

    def residual_tile(t):
        i0 = pl.multiple_of(t * SUB, SUB)
        e = [jnp.exp(logit[a, pl.ds(i0, SUB), :]) for a in range(states)]
        total = functools.reduce(lambda x, y: x + y, e)
        s = seq_ref[pl.ds(i0, SUB), :]
        w = weight_ref[...]
        lane = iota((SUB, states), 1)
        field = jnp.zeros((SUB, states), f32)
        for a in range(states):
            r = w * (e[a] / total - (s == a).astype(f32))
            res[a, pl.ds(i0, SUB), :] = r
            field = jnp.where(lane == a, jnp.sum(r, axis=1, keepdims=True), field)
        gfield_ref[pl.ds(i0, SUB), :] = field
    loop(0, rows // SUB, residual_tile, 4)
    back = remote(res.at[:, pl.ds(0, band), :], res_in, h_send.at[2], h_recv.at[2], prv)
    back.start()

    lane = iota((SUB, LANES), 1)
    local = iota((SUB, LANES), 0)
    column = []
    for v in range(nv):
        col = lane + v * LANES
        for a in range(states - 1, 0, -1):
            if a * states <= v * LANES:
                col = lane + (v * LANES - a * states)
                first = a
                break
        else:
            first = 0
        for a in range(first + 1, states):
            if a * states < (v + 1) * LANES:
                col = jnp.where(lane + v * LANES >= a * states, lane + (v * LANES - a * states), col)
        column.append(col & (PAD - 1))

    def assemble(source, w):
        off = local + (w - 1)
        first = (w - 1) // PER
        steps = (w - 1 + SUB - 1) // PER - first
        chosen = {}

        def chosen_rows(a):
            if a not in chosen:
                x = source(a, first)
                for k in range(1, steps + 1):
                    x = jnp.where(off >= (first + k) * PER, source(a, first + k), x)
                chosen[a] = x
            return chosen[a]

        outs = []
        for v in range(nv):
            index = (off & (PER - 1)) * PAD + column[v]
            out = None
            for a in range(states):
                if a * states >= (v + 1) * LANES or (a + 1) * states <= v * LANES:
                    continue
                got = lookup(chosen_rows(a), index)
                out = got if out is None else jnp.where(lane + v * LANES >= a * states, got, out)
            outs.append(out)
        return outs

    for a in range(states):
        hi, lo = split(res[a])
        both = jnp.concatenate([hi, lo], axis=1)
        x = dot(pick_st, both)
        rs[a] = x[:, :seqs] + x[:, seqs:]
        x = dot(pick_et, both)
        rej[pl.ds(a, slots, stride=PAD), :] = x[:, :seqs] + x[:, seqs:]

    def hot_rows(s):
        return jnp.concatenate([(s == a).astype(f32) for a in range(states)], axis=0).astype(bf16)

    def hot_columns(s):
        level = iota((PAD, seqs), 0)
        return jnp.concatenate(
            [(s[r : r + 1] == level).astype(f32) for r in range(s.shape[0])], axis=0).astype(bf16)

    def pick_from(d):
        return lambda a, v: d[a * SUB : (a + 1) * SUB, v * LANES : (v + 1) * LANES]

    def far_half(t):
        s_start = tile_of(recv, t, flat, flat + seqs).astype(i32)
        left = hot_rows(s_start)
        hi, lo = split(rej[pl.ds(pl.multiple_of(t * SUB * PAD, SUB * PAD), SUB * PAD), :])
        d = dot_nt(left, hi) + dot_nt(left, lo)
        for v, x in enumerate(assemble(pick_from(d), 1)):
            put_tile(gsend, t, v * LANES, (v + 1) * LANES, x)

    if depth == SUB:
        loop(1, n, lambda k: far_half(peer(k)), 5, lambda k: gradient(k).start())
        far_half(me)
    else:
        loop(0, tiles, far_half, 4)
        loop(1, n, lambda k: gradient(k).start())
    grecv[me] = gsend[me]

    def near_half(t):
        s_end = tile_of(recv, t, flat + seqs, flat + 2 * seqs).astype(i32)
        right = hot_columns(s_end)
        at = pl.multiple_of(t * SUB, SUB)
        hi, lo = split(rs[:, pl.ds(at, SUB), :].reshape(states * SUB, seqs))
        d = dot_nt(hi, right) + dot_nt(lo, right)
        for v, x in enumerate(assemble(pick_from(d), 1)):
            put_tile(gown, t, v * LANES, (v + 1) * LANES, x)
    loop(0, tiles, near_half, 4)

    for a in range(states):
        rj[pl.ds(a, rows, stride=PAD), :] = res[a]
    back.wait_recv()
    for a in range(states):
        rj[pl.ds(rows * PAD + a, band, stride=PAD), :] = res_in[a]

    def columns_of(t):
        h = hot_columns(seqx[pl.ds(pl.multiple_of(t * SUB, SUB), SUB), :])
        at = pl.multiple_of(t * SUB * PAD, SUB * PAD)
        hi, lo = split(rj[pl.ds(at, SUB * PAD), :])
        xhi[pl.ds(at, SUB * PAD), :] = jnp.concatenate([h, hi], axis=1)
        xlo[pl.ds(at, SUB * PAD), :] = jnp.concatenate([h, lo], axis=1)
    loop(0, (rows + band) // SUB, columns_of, 2)
    reached = dband.shape[2]

    def band_product(t):
        i0 = t * SUB
        hi, lo = split(res[:, pl.ds(i0, SUB), :].reshape(states * SUB, seqs))
        h = hot_rows(seq_ref[pl.ds(i0, SUB), :])
        at = pl.ds((i0 + 1) * PAD, reached)
        dband[t % 2] = dot_nt(jnp.concatenate([hi, h], axis=1), xhi[at, :]) + dot_nt(
            jnp.concatenate([lo, h], axis=1), xlo[at, :])

    def band_tile(t):
        def source(a, v):
            return dband[t % 2, pl.ds(a * SUB, SUB), v * LANES : (v + 1) * LANES]
        for w in range(1, band + 1):
            for v, x in enumerate(assemble(source, w)):
                g4[v, pl.ds(t * SUB * band + w - 1, SUB, stride=band), :] = x

    band_product(0)
    for t in range(rows // SUB):
        if t + 1 < rows // SUB:
            band_product(t + 1)
        band_tile(t)

    for v in range(nv):
        width = min(LANES, square - v * LANES)
        gband_ref[:, v * LANES : v * LANES + width] = jnp.where(
            exists[:, :width], g4[v, :, :width], 0.0)

    loop(1, n, lambda k: gradient(k).wait_recv())
    gcontact_ref[...] = gown[:, :, :square] + grecv[:, :, :square]

    halo.wait_send()
    spill.wait_send()
    back.wait_send()

    def drain(k):
        message(k).wait_send()
        gradient(k).wait_send()
    loop(1, n, drain)


def on_device(sequences, fields, band_coupling, contact_coupling, slot_start, slot_end, seq_weight):
    rows, seqs = sequences.shape
    states = fields.shape[1]
    band = band_coupling.shape[1]
    n, depth = contact_coupling.shape[1:3]
    square = states * states
    slots = n * depth
    nv = -(-square // LANES)
    flat = nv * LANES
    flip = flip_matrix(states, flat)
    nt = flip.shape[1] // LANES
    near = SUB + band - 1
    reached = -(-near // SUB) * SUB * PAD
    columns = (rows - SUB + 1) * PAD + reached
    V = pltpu.VMEM
    scratch = [
        V((nv, rows * band, LANES), f32),
        V((nt, (rows + 2 * band) * band, LANES), f32),
        V((rows + 2 * band, seqs), i32),
        V((band, seqs), i32),
        V((rows + band, seqs), i32),
        V((n, depth, flat + 2 * seqs), f32),
        V((n, depth, flat + 2 * seqs), f32),
        V((states, 2 * slots, seqs), f32),
        V((nt, slots, LANES), f32),
        V((states, rows, seqs), f32),
        V((states, band, seqs), f32),
        V((states, band, seqs), f32),
        V((states, rows, seqs), f32),
        V((states, band, seqs), f32),
        V((columns, 2 * seqs), bf16),
        V((columns, 2 * seqs), bf16),
        V(((rows + band) * PAD, seqs), f32),
        V((states, slots, seqs), f32),
        V((slots * PAD, seqs), f32),
        V((2, states * SUB, reached), f32),
        V((nv, rows * band, LANES), f32),
        V((n, depth, flat), f32),
        V((n, depth, flat), f32),
        V((n, depth, flat), f32),
        pltpu.SemaphoreType.DMA((n,)),
        pltpu.SemaphoreType.DMA((n,)),
        pltpu.SemaphoreType.DMA((n,)),
        pltpu.SemaphoreType.DMA((n,)),
        pltpu.SemaphoreType.DMA((3,)),
        pltpu.SemaphoreType.DMA((3,)),
    ]
    operands = (
        sequences,
        slot_start.reshape(1, slots),
        slot_end.reshape(1, slots),
        contact_coupling[0],
        band_coupling.reshape(rows * band, square),
        jnp.asarray(flip, bf16),
        fields,
        seq_weight.reshape(1, seqs),
    )
    scratch += [V(x.shape, x.dtype) for x in operands]
    scratch.append(pltpu.SemaphoreType.DMA((len(operands),)))
    gband, gcontact, gfield = pl.pallas_call(
        functools.partial(kernel, n, depth, band),
        out_shape=(
            jax.ShapeDtypeStruct((rows * band, square), f32),
            jax.ShapeDtypeStruct((n, depth, square), f32),
            jax.ShapeDtypeStruct((rows, states), f32),
        ),
        in_specs=[pl.BlockSpec(memory_space=pl.ANY)] * len(operands),
        out_specs=(pl.BlockSpec(memory_space=V),) * 3,
        scratch_shapes=scratch,
        compiler_params=pltpu.CompilerParams(
            collective_id=0, has_side_effects=True, vmem_limit_bytes=58 * 2**20),
    )(*operands)
    return gband.reshape(rows, band, square), gcontact[None], gfield


def solution(mesh):
    in_specs = (
        P(("grp", "pos"), None),
        P(("grp", "pos"), None),
        P(("grp", "pos"), None, None),
        P(("grp", "pos"), None, None, None),
        P(("grp", "pos"), None, None),
        P(("grp", "pos"), None, None),
        P("grp"),
    )
    out_specs = (
        P(("grp", "pos"), None, None),
        P(("grp", "pos"), None, None, None),
        P(("grp", "pos"), None),
    )
    return jax.shard_map(
        on_device, mesh=mesh, in_specs=in_specs, out_specs=out_specs, check_vma=False
    )
```
